256 devices in a mesh: ctx: 64 (over y, z, core), head: 4 (over x).
Axes of the slice: x: 4, y: 4, z: 8, core: 2. Of those that a mesh axis runs over, the one named last changes fastest.
Arguments:
- tokens_in: bfloat16 [8192, 12288], P('ctx'), may hold values from -16 to 16
- w_key: bfloat16 [12288, 512], P('ctx', 'head'), may hold values from -0.0546875 to 0.0546875
- w_value: bfloat16 [12288, 512], P('ctx', 'head'), may hold values from -0.0546875 to 0.0546875
- queries: bfloat16 [8192, 6144], P('ctx', 'head'), may hold values from -140 to 140
- out_grad: bfloat16 [8192, 6144], P('ctx', 'head'), may hold values from -24 to 24
- attn_out: bfloat16 [8192, 6144], P('ctx', 'head'), may hold values from -6 to 6
- doc_ids: int32 [8192], P('ctx'), may hold values from 0 to 2, never falling along the last dimension, each value on 1 to 6144 neighbouring positions
Outputs:
- grad_wk: float32 [12288, 512], P('ctx', 'head')
- grad_wv: float32 [12288, 512], P('ctx', 'head')
- input_grad: float32 [8192, 12288], P('ctx', 'head')
The draws below stay inside these ranges and needn't reach their ends.
All inputs are finite; a program needn't handle non-finite values.
Results may differ from the reference program's by a relative error of at most 0.017.
Values may be sent and summed in bfloat16 or wider, within the bound.
No kernel may reach another device: no remote copies, remote signals or barrier semaphores. Data moves between devices by JAX's collectives and lax.ppermute only.
A program may use at most 128 MiB of HBM per device.

```python
import math
import jax
import jax.numpy as jnp
import numpy as np
from jax import lax

D = 12288
HD = 128
QH = 48
KVH = 4
WINDOW = 4096
TOKENS = 8192


def draw_queries(key, part):
    key = jax.random.fold_in(key, 11)
    first = jax.random.fold_in(key, 0)
    return jnp.clip(jax.random.normal(first, (TOKENS, QH * HD), jnp.float32), -6.0, 6.0).astype(jnp.bfloat16)


def spiked(array, own_key, source, target, parts, factor):
    owner, partner = [(jnp.arange(array.shape[position]) // (array.shape[position] // parts)).reshape([-1 if axis == position else 1 for axis in range(array.ndim)]) for position in (source, target)]
    chosen = jax.random.permutation(own_key, parts)[partner]
    strong = (owner == chosen) | (owner == (partner + parts // 2) % parts)
    return jnp.where(strong, factor * array, array)


def levels(stream_key, dims, pieces, smallest, largest):
    def one(axis_at, parts):
        draws = jax.random.uniform(jax.random.fold_in(jax.random.fold_in(stream_key, 6), axis_at), (parts,), jnp.float32, smallest / len(pieces), largest / len(pieces))
        return jnp.repeat(jnp.exp(draws), dims[axis_at] // parts).reshape((-1,) + (1,) * (len(dims) - axis_at - 1))

    level = one(*pieces[0])
    for cut in pieces[1:]:
        level = level * one(*cut)
    return level


def profile(amount, total, bound, slope):
    weights = [(1 << 20) // math.isqrt(standing ** slope) + 1 for standing in range(2, amount + 1)]
    surplus, holding = total - bound - (amount - 1), [1] * (amount - 1)
    while surplus > 0:
        free = [i for i in range(amount - 1) if holding[i] < bound]
        mass, remaining = sum([weights[i] for i in free]), surplus
        for i in free:
            more = min(bound - holding[i], max(1, remaining * weights[i] // mass), surplus)
            holding[i] = holding[i] + more
            surplus = surplus - more
    return np.array([bound] + holding)


def uneven(key, number_of, total, most, slope):
    if number_of == 2:
        one = jax.random.randint(key, (), max(1, total - most), min(most, total - 1) + 1)
        return jnp.stack([one, total - one])
    tallies = jnp.asarray(profile(number_of, total, most, slope), jnp.int32)
    couples = (number_of - 1) // 2
    giver, taker = tallies[1:1 + 2 * couples:2], tallies[2:2 + 2 * couples:2]
    margin = jnp.minimum(giver - 1, most - taker)
    passed = jax.random.randint(jax.random.fold_in(key, 1), (couples,), 0, 1 << 20) % (margin + 1)
    tallies = tallies.at[1:1 + 2 * couples:2].set(giver - passed).at[2:2 + 2 * couples:2].set(taker + passed)
    return tallies[jax.random.permutation(jax.random.fold_in(key, 2), number_of)]


def bell_draw(stream_key, extent, deviation, reach, pieces=(), kind=jnp.bfloat16):
    entries = jax.random.normal(stream_key, extent, jnp.float32) * deviation
    if len(pieces) > 0:
        entries = levels(stream_key, extent, pieces, -0.22, 0.18) * entries
    return jnp.clip(entries, min=-reach, max=reach).astype(kind)


def gaussian_with(key, dims, scale, bound, shards, heavy, kind=jnp.bfloat16):
    array = scale * jax.random.normal(key, dims, jnp.float32)
    if shards:
        array = array * levels(key, dims, shards, -0.22, 0.18)
    return jnp.clip(spiked(array, jax.random.fold_in(key, 3), *heavy), -bound, bound).astype(kind)


def setup_inputs(seed: int = 0) -> dict:
    splits = jax.random.split(jax.random.key(seed), 8)
    tokens_in = gaussian_with(splits[0], (TOKENS, D), 1.0, 16.0, ((0, 64),), (0, 1, 64, 4.0))
    w_key = bell_draw(splits[1], (D, KVH * HD), D ** -0.5, 0.0546875, ((0, 64), (1, 4)))
    w_value = bell_draw(splits[2], (D, KVH * HD), D ** -0.5, 0.0546875, ((0, 64), (1, 4)))
    queries = draw_queries(jax.random.fold_in(splits[7], 71), 0)
    out_grad = bell_draw(splits[4], (TOKENS, QH * HD), 4.0, 24.0, ((0, 64), (1, 4)))
    attn_out = bell_draw(splits[5], (TOKENS, QH * HD), 1.0, 6.0, ((0, 64), (1, 4)))
    doc_ids = jnp.searchsorted(jnp.cumsum(uneven(splits[6], 3, TOKENS, 3 * TOKENS // 4, 0)), jnp.arange(TOKENS), side="right").astype(jnp.int32)
    return dict(tokens_in=tokens_in, w_key=w_key, w_value=w_value, queries=queries, out_grad=out_grad, attn_out=attn_out, doc_ids=doc_ids)


def reference(tokens_in, w_key, w_value, queries, out_grad, attn_out, doc_ids):
    group = QH // KVH
    scale = 1.0 / math.sqrt(HD)
    block = math.gcd(512, TOKENS)
    span = WINDOW + block
    both = jnp.concatenate((w_key, w_value), 1)
    kv = jnp.dot(tokens_in, both, preferred_element_type=jnp.float32).astype(jnp.bfloat16)
    keys = kv[:, :KVH * HD].astype(jnp.float32).reshape(TOKENS, KVH, HD)
    values = kv[:, KVH * HD:].astype(jnp.float32).reshape(TOKENS, KVH, HD)
    query_all = queries.astype(jnp.float32).reshape(TOKENS, KVH, group, HD)
    grad_all = out_grad.astype(jnp.float32).reshape(TOKENS, KVH, group, HD)
    delta = lax.optimization_barrier(jnp.sum(grad_all * attn_out.astype(jnp.float32).reshape(TOKENS, KVH, group, HD), -1))
    seg_pad = jnp.concatenate((jnp.full((WINDOW,), -1, jnp.int32), doc_ids.astype(jnp.int32)))
    key_parts = []
    value_parts = []
    for kv_head in range(KVH):
        key_pad = jnp.concatenate((jnp.zeros((WINDOW, HD), jnp.float32), keys[:, kv_head]))
        value_pad = jnp.concatenate((jnp.zeros((WINDOW, HD), jnp.float32), values[:, kv_head]))
        query_head = query_all[:, kv_head]
        grad_head = grad_all[:, kv_head]
        delta_head = delta[:, kv_head]

        def step(carry, index):
            dk_acc, dv_acc = carry
            start = (index * block).astype(jnp.int32)
            qb = lax.dynamic_slice_in_dim(query_head, start, block, 0)
            ob = lax.dynamic_slice_in_dim(grad_head, start, block, 0)
            db = lax.dynamic_slice_in_dim(delta_head, start, block, 0)
            qseg = lax.dynamic_slice_in_dim(doc_ids.astype(jnp.int32), start, block, 0)
            kb = lax.dynamic_slice_in_dim(key_pad, start, span, 0)
            vb = lax.dynamic_slice_in_dim(value_pad, start, span, 0)
            kseg = lax.dynamic_slice_in_dim(seg_pad, start, span, 0)
            qpos = start + jnp.arange(block, dtype=jnp.int32)
            kpos = start - WINDOW + jnp.arange(span, dtype=jnp.int32)
            visible = (kpos[None, :] <= qpos[:, None]) & (qpos[:, None] - kpos[None, :] < WINDOW)
            visible = visible & (kpos[None, :] >= 0) & (kseg[None, :] == qseg[:, None])
            scores = jnp.einsum('tjd,kd->jtk', qb, kb) * scale
            scores = jnp.where(visible[None], scores, -jnp.inf)
            top = lax.optimization_barrier(jnp.max(scores, -1, keepdims=True))
            weights = jnp.exp(scores - top)
            weights = weights / lax.optimization_barrier(jnp.sum(weights, -1, keepdims=True))
            rounded = lax.optimization_barrier(weights.astype(jnp.bfloat16)).astype(jnp.float32)
            dv_part = jnp.einsum('jtk,tjd->kd', rounded, ob)
            dp = jnp.einsum('tjd,kd->jtk', ob, vb)
            ds = weights * (dp - db.T[:, :, None])
            ds = lax.optimization_barrier(ds.astype(jnp.bfloat16)).astype(jnp.float32)
            dk_part = jnp.einsum('jtk,tjd->kd', ds, qb) * scale
            dk_acc = lax.dynamic_update_slice_in_dim(dk_acc, lax.dynamic_slice_in_dim(dk_acc, start, span, 0) + dk_part, start, 0)
            dv_acc = lax.dynamic_update_slice_in_dim(dv_acc, lax.dynamic_slice_in_dim(dv_acc, start, span, 0) + dv_part, start, 0)
            return ((dk_acc, dv_acc), None)
        empty = jnp.zeros((WINDOW + TOKENS, HD), jnp.float32)
        (dk_acc, dv_acc), _ = lax.scan(step, (empty, empty), jnp.arange(TOKENS // block, dtype=jnp.int32))
        key_parts.append(dk_acc[WINDOW:])
        value_parts.append(dv_acc[WINDOW:])
    dk_all = jnp.concatenate(key_parts, 1).astype(jnp.bfloat16)
    dv_all = jnp.concatenate(value_parts, 1).astype(jnp.bfloat16)
    contract = (((0,), (0,)), ((), ()))
    grad_wk = lax.dot_general(tokens_in, dk_all, contract, preferred_element_type=jnp.float32)
    grad_wv = lax.dot_general(tokens_in, dv_all, contract, preferred_element_type=jnp.float32)
    across = (((1,), (1,)), ((), ()))
    input_grad = lax.dot_general(dk_all, w_key, across, preferred_element_type=jnp.float32)
    input_grad = input_grad + lax.dot_general(dv_all, w_value, across, preferred_element_type=jnp.float32)
    return (grad_wk, grad_wv, input_grad)
```

```python
import math

import jax
import jax.numpy as jnp
from jax import lax
from jax.experimental import pallas as pl
from jax.experimental.pallas import tpu as pltpu
from jax.sharding import Mesh
from jax.sharding import PartitionSpec as P

HD = 128
WINDOW = 4096
ROWS = 128
PAIR = 2 * ROWS
RING = 8
PLANE = RING * ROWS
CHUNKS = WINDOW // PAIR + 1
SPAN = CHUNKS * PAIR
GROUP = 4
TILE = GROUP * ROWS
SCALE = 1.0 / math.sqrt(HD)
RATE = SCALE * math.log2(math.e)
HIDDEN = -1e30

NT = (((1,), (1,)), ((), ()))
NN = (((1,), (0,)), ((), ()))
TN = (((0,), (0,)), ((), ()))


def dot(a, b, dims):
    return lax.dot_general(a, b, dims, preferred_element_type=jnp.float32)


def attend(
    place, own0, own1, own2, far0, far1, far2, q_ref, o_ref, delta_ref, doc_ref,
    near_out, far_out, k_s, v_s, p_s, m_s, dk_s, dv_s,
):
    z = place[0]
    c = place[1]
    odd = place[2]
    planes = ((own0, far0), (own1, far1), (own2, far2))
    for plane, pair in enumerate(planes):

        @pl.loop(0, RING)
        def load(step, plane=plane, pair=pair):
            j = plane * RING + step + odd * (1 - 2 * (step % 2)) - z

            @pl.when((j >= 0) & (j < CHUNKS))
            def _():
                for slot, ref in enumerate(pair):
                    core = c if slot == 0 else 1 - c
                    src = pl.ds(pl.multiple_of(step * ROWS, ROWS), ROWS)
                    dst = pl.ds(pl.multiple_of(j * PAIR + core * ROWS, ROWS), ROWS)
                    k_s[dst, :] = ref[src, :HD]
                    v_s[dst, :] = ref[src, HD:]

    doc = doc_ref[...]
    token = c * ROWS + lax.broadcasted_iota(jnp.int32, (1, TILE), 1) % ROWS
    high = token + WINDOW
    start = jnp.where(doc == 0, place[3], jnp.where(doc == 1, place[4], place[5]))
    low = jnp.maximum(start, token + 1)
    row = lax.broadcasted_iota(jnp.int32, (PAIR, TILE), 0)

    for g in range(q_ref.shape[0] // TILE):
        q = q_ref[g * TILE : (g + 1) * TILE, :]
        o = o_ref[g * TILE : (g + 1) * TILE, :]
        delta = delta_ref[g]

        def first(j, carry, q=q):
            top, total = carry
            at = pl.ds(pl.multiple_of(j * PAIR, PAIR), PAIR)
            s = dot(k_s[at, :], q, NT)
            seen = (row >= low - j * PAIR) & (row <= high - j * PAIR)
            s = jnp.where(seen, s, HIDDEN)
            peak = jnp.maximum(top, jnp.max(s, 0, keepdims=True))
            p = jnp.exp2((s - peak) * RATE)
            p_s[at, :] = p
            m_s[j] = peak
            total = total * jnp.exp2((top - peak) * RATE) + jnp.sum(p, 0, keepdims=True)
            return peak, total

        top, total = lax.fori_loop(
            0,
            CHUNKS,
            first,
            (jnp.full((1, TILE), HIDDEN, jnp.float32), jnp.zeros((1, TILE), jnp.float32)),
        )
        share = 1.0 / total

        def second(j, carry, g=g, q=q, o=o, delta=delta, top=top, share=share):
            at = pl.ds(pl.multiple_of(j * PAIR, PAIR), PAIR)
            p = p_s[at, :] * (jnp.exp2((m_s[j] - top) * RATE) * share)
            dp = dot(v_s[at, :], o, NT)
            ds = (p * (dp - delta)).astype(jnp.bfloat16)
            dv = dot(p.astype(jnp.bfloat16), o, NN)
            dk = dot(ds, q, NN)
            if g == 0:
                dv_s[at, :] = dv
                dk_s[at, :] = dk
            else:
                dv_s[at, :] += dv
                dk_s[at, :] += dk
            return carry

        lax.fori_loop(0, CHUNKS, second, 0)

    for plane in range(3):

        @pl.loop(0, RING)
        def store(step, plane=plane):
            j = plane * RING + step + odd * (1 - 2 * (step % 2)) - z
            block = plane * RING + step + odd * (1 - 2 * (step % 2))
            dst = pl.ds(pl.multiple_of(block * ROWS, ROWS), ROWS)
            inside = (j >= 0) & (j < CHUNKS)

            @pl.when(inside)
            def _():
                for slot, ref in enumerate((near_out, far_out)):
                    core = c if slot == 0 else 1 - c
                    src = pl.ds(pl.multiple_of(j * PAIR + core * ROWS, ROWS), ROWS)
                    ref[dst, :HD] = (dk_s[src, :] * SCALE).astype(jnp.bfloat16)
                    ref[dst, HD:] = dv_s[src, :].astype(jnp.bfloat16)

            @pl.when(jnp.logical_not(inside))
            def _():
                for ref in (near_out, far_out):
                    ref[dst, :] = jnp.zeros((ROWS, 2 * HD), jnp.bfloat16)


def attention(place, kv, q, o, delta, doc):
    out = jax.ShapeDtypeStruct((3 * PLANE, 2 * HD), jnp.bfloat16)
    heads = q.shape[0] // ROWS
    vmem = pl.BlockSpec(memory_space=pltpu.VMEM)
    return pl.pallas_call(
        attend,
        out_shape=(out, out),
        in_specs=[pl.BlockSpec(memory_space=pltpu.SMEM)] + [vmem] * 10,
        out_specs=(vmem, vmem),
        scratch_shapes=[
            pltpu.VMEM((SPAN, HD), jnp.bfloat16),
            pltpu.VMEM((SPAN, HD), jnp.bfloat16),
            pltpu.VMEM((SPAN, TILE), jnp.float32),
            pltpu.VMEM((CHUNKS, 1, TILE), jnp.float32),
            pltpu.VMEM((SPAN, HD), jnp.float32),
            pltpu.VMEM((SPAN, HD), jnp.float32),
        ],
        compiler_params=pltpu.CompilerParams(vmem_limit_bytes=48 << 20),
        cost_estimate=pl.CostEstimate(
            flops=8 * heads * ROWS * SPAN * HD,
            bytes_accessed=8 << 20,
            transcendentals=heads * ROWS * SPAN,
        ),
        name="attend",
    )(place, *kv, q, o, delta, doc)


def project(rows_ref, key_ref, value_ref, sent, w_s):
    depth = value_ref.shape[1]
    blocks = value_ref.shape[0]
    counts = jnp.zeros((8, HD), jnp.float32)
    for i in range(blocks):
        w_s[i * depth : (i + 1) * depth, :HD] = key_ref[i, :depth, :]
        w_s[i * depth : (i + 1) * depth, HD:] = value_ref[i]
        counts = counts + key_ref[i, depth:, :].astype(jnp.float32)[:8]
    rows = rows_ref[...].reshape(-1, rows_ref.shape[2])
    places = rows_ref.shape[0]
    sent[:, :ROWS, :] = dot(rows, w_s[...], NN).reshape(places, ROWS, 2 * HD)
    sent[:, ROWS:, :HD] = jnp.broadcast_to(counts[None], (places, 8, HD))
    sent[:, ROWS:, HD:] = jnp.zeros((places, 8, HD), jnp.float32)


def weight_terms(core, rows_ref, terms_ref, near, far):
    c = core[0]
    depth = near.shape[1]
    terms = terms_ref[...]
    for z in range(RING):
        cols = rows_ref[:, :, z * 2 * depth : (z + 1) * 2 * depth]
        block = dot(cols.reshape(-1, 2 * depth), terms, TN)
        lower, upper = block[:depth], block[depth:]
        near[z] = jnp.where(c == 0, lower, upper)
        far[z] = jnp.where(c == 0, upper, lower).astype(jnp.bfloat16)


def input_terms(terms_ref, w_ref, out):
    heads, width = w_ref.shape[:2]
    step = 512
    for n in range(0, width, step):
        total = dot(terms_ref[0], w_ref[0, n : n + step, :], NT)
        for h in range(1, heads):
            total = total + dot(terms_ref[h], w_ref[h, n : n + step, :], NT)
        out[:, n : n + step] = total


def kernel_call(f, out_shape, inputs, scratch=(), flops=0):
    smem, vmem = pl.BlockSpec(memory_space=pltpu.SMEM), pl.BlockSpec(memory_space=pltpu.VMEM)
    return pl.pallas_call(
        f,
        out_shape=out_shape,
        in_specs=[smem if a.ndim == 1 else vmem for a in inputs],
        out_specs=jax.tree.map(lambda _: vmem, out_shape),
        scratch_shapes=scratch,
        compiler_params=pltpu.CompilerParams(vmem_limit_bytes=40 << 20),
        cost_estimate=pl.CostEstimate(flops=flops, bytes_accessed=8 << 20, transcendentals=0),
        name=f.__name__,
    )(*inputs)


def split_columns(a, parts):
    rows, width = a.shape[0], a.shape[1] // parts

    def move(src, dst):
        dst[0] = src[...]

    return pl.pallas_call(
        move,
        grid=(parts,),
        out_shape=jax.ShapeDtypeStruct((parts, rows, width), a.dtype),
        in_specs=[pl.BlockSpec((rows, width), lambda i: (0, i))],
        out_specs=pl.BlockSpec((1, rows, width), lambda i: (i, 0, 0)),
        name="split_columns",
    )(a)


def swap(a, axis="c"):
    return lax.ppermute(a, axis, [(0, 1), (1, 0)])


def body(tokens_in, w_key, w_value, queries, out_grad, attn_out, doc_ids):
    f32, bf16 = jnp.float32, jnp.bfloat16
    heads = queries.shape[1] // HD
    y, zb, za, c = (lax.axis_index(name) for name in ("y", "zb", "za", "c"))
    z = zb * 2 + za
    ys = lax.axis_size("y")
    xs = lax.axis_size("x")
    depth = w_key.shape[0]
    model = tokens_in.shape[1]
    shape = jax.ShapeDtypeStruct
    core = c.astype(jnp.int32)[None]
    place = jnp.stack([z, c, za]).astype(jnp.int32)

    cut = split_columns(tokens_in, ys)
    rows_y = lax.all_to_all(cut, "y", 0, 0)

    turned = lax.ppermute(
        jnp.concatenate((w_key, w_value), 1),
        ("y", "x"),
        [(a * xs + b, b * xs + a) for a in range(ys) for b in range(xs)],
    )

    before = jnp.stack([jnp.sum(doc_ids < 1), jnp.sum(doc_ids < 2)]).astype(f32)
    counts = jnp.zeros((16, HD), f32).at[0, :2].set(before).astype(bf16)
    plane_axes = ("zb", "za", "c")
    key_part = lax.all_gather(jnp.concatenate((w_key, counts), 0), plane_axes, axis=0)
    key_part, tied = lax.optimization_barrier((key_part, w_value))
    value_part = lax.all_gather(tied, plane_axes, axis=0)

    def by_head(a):
        return a.reshape(ROWS, heads, HD).swapaxes(0, 1)

    delta = jnp.sum(
        out_grad.astype(f32).reshape(ROWS, heads, HD)
        * attn_out.astype(f32).reshape(ROWS, heads, HD),
        -1,
    )
    delta = delta.T.reshape(heads // GROUP, 1, TILE)
    doc_tile = jnp.tile(doc_ids, GROUP)[None]
    q_rows = by_head(queries).reshape(heads * ROWS, HD)
    o_rows = by_head(out_grad).reshape(heads * ROWS, HD)

    quarter = model // ys
    sent = kernel_call(
        project,
        shape((ys, ROWS + 8, 2 * HD), f32),
        (rows_y, key_part, value_part),
        [pltpu.VMEM((quarter, 2 * HD), bf16)],
        2 * ys * ROWS * quarter * 2 * HD,
    )
    got = lax.all_to_all(sent, "y", 0, 0)
    kv = jnp.sum(got[:, :ROWS], 0).astype(bf16)
    starts = jnp.sum(got[:, ROWS], 0)

    origin = (y * RING + z - WINDOW // PAIR) * PAIR
    starts = jnp.concatenate((jnp.zeros((1,), jnp.int32), starts[:2].astype(jnp.int32)))
    window = jnp.concatenate((place, starts - origin))

    turned, _ = lax.optimization_barrier((turned, kv))
    w_all = lax.all_gather(turned, ("y", "zb", "za", "c"), axis=0, tiled=True)
    w_all = w_all.reshape(xs, quarter, 2 * HD)

    pair = jnp.concatenate((kv, swap(kv, "za")), 0)
    own2 = lax.all_gather(pair, "zb", axis=0, tiled=True)
    own1 = lax.ppermute(own2, "y", [(i, i + 1) for i in range(ys - 1)])
    own0 = lax.ppermute(own2, "y", [(i, i + 2) for i in range(ys - 2)])
    far2, far1, far0 = swap(own2), swap(own1), swap(own0)

    near, far = attention(
        window, (own0, own1, own2, far0, far1, far2), q_rows, o_rows, delta, doc_tile
    )

    mine = near.astype(f32) + swap(far).astype(f32)
    from1 = lax.ppermute(
        mine[PLANE : 2 * PLANE].astype(bf16), "y", [(i + 1, i) for i in range(ys - 1)]
    )
    from2 = lax.ppermute(mine[:PLANE].astype(bf16), "y", [(i + 2, i) for i in range(ys - 2)])
    summed = mine[2 * PLANE :] + from1.astype(f32) + from2.astype(f32)
    parts = lax.all_to_all(
        summed.astype(bf16).reshape(RING, ROWS, 2 * HD), ("zb", "za"), 0, 0
    )
    grad_terms = jnp.sum(parts.astype(f32), 0).astype(bf16)

    terms_y = lax.all_gather(grad_terms, "y", axis=0, tiled=True)
    dims = (RING, depth, 2 * HD)
    near, far = kernel_call(
        weight_terms,
        (shape(dims, f32), shape(dims, bf16)),
        (core, rows_y, terms_y),
        (),
        2 * ys * ROWS * quarter * 2 * HD,
    )
    summed = (near + swap(far).astype(f32)).astype(bf16)
    parts = lax.all_to_all(summed, ("zb", "za"), 0, 0)
    grads = jnp.sum(parts.astype(f32), 0)

    terms_x = lax.all_gather(grad_terms, "x", axis=0)
    input_grad = kernel_call(
        input_terms,
        shape((ROWS, quarter), f32),
        (terms_x, w_all),
        (),
        2 * ROWS * quarter * xs * 2 * HD,
    )
    return (grads[:, :HD], grads[:, HD:], input_grad)


def solution(mesh):
    fine = Mesh(
        mesh.devices.reshape(4, RING // 2, 2, 2, 4), ("y", "zb", "za", "c", "x")
    )
    ctx = ("y", "zb", "za", "c")
    split = P(ctx, "x")
    return jax.shard_map(
        body,
        mesh=fine,
        in_specs=(P(ctx, None), split, split, split, split, split, P(ctx)),
        out_specs=(split, split, split),
        check_vma=False,
    )
```

```python
import math

import jax
import jax.numpy as jnp
from jax import lax
from jax.experimental import pallas as pl
from jax.experimental.pallas import tpu as pltpu
from jax.sharding import Mesh
from jax.sharding import PartitionSpec as P

HD = 128
WINDOW = 4096
ROWS = 128
PAIR = 2 * ROWS
RING = 8
PLANE = RING * ROWS
CHUNKS = WINDOW // PAIR + 1
SPAN = CHUNKS * PAIR
GROUP = 4
TILE = GROUP * ROWS
SCALE = 1.0 / math.sqrt(HD)
RATE = SCALE * math.log2(math.e)
HIDDEN = -1e30

NT = (((1,), (1,)), ((), ()))
NN = (((1,), (0,)), ((), ()))
TN = (((0,), (0,)), ((), ()))


def dot(a, b, dims):
    return lax.dot_general(a, b, dims, preferred_element_type=jnp.float32)


def attend(
    place, own0, own1, own2, far0, far1, far2, q_ref, o_ref, delta_ref, doc_ref,
    near_out, far_out, k_s, v_s, p_s, m_s, dk_s, dv_s,
):
    z = place[0]
    c = place[1]
    odd = place[2]
    planes = ((own0, far0), (own1, far1), (own2, far2))
    for plane, pair in enumerate(planes):

        @pl.loop(0, RING)
        def load(step, plane=plane, pair=pair):
            j = plane * RING + step + odd * (1 - 2 * (step % 2)) - z

            @pl.when((j >= 0) & (j < CHUNKS))
            def _():
                for slot, ref in enumerate(pair):
                    core = c if slot == 0 else 1 - c
                    src = pl.ds(pl.multiple_of(step * ROWS, ROWS), ROWS)
                    dst = pl.ds(pl.multiple_of(j * PAIR + core * ROWS, ROWS), ROWS)
                    k_s[dst, :] = ref[src, :HD]
                    v_s[dst, :] = ref[src, HD:]

    doc = doc_ref[...]
    token = c * ROWS + lax.broadcasted_iota(jnp.int32, (1, TILE), 1) % ROWS
    high = token + WINDOW
    start = jnp.where(doc == 0, place[3], jnp.where(doc == 1, place[4], place[5]))
    low = jnp.maximum(start, token + 1)
    row = lax.broadcasted_iota(jnp.int32, (PAIR, TILE), 0)
    dk_s[...] = jnp.zeros_like(dk_s)
    dv_s[...] = jnp.zeros_like(dv_s)

    @pl.loop(0, q_ref.shape[0] // TILE)
    def heads(g):
        tile = pl.ds(pl.multiple_of(g * TILE, TILE), TILE)
        q = q_ref[tile, :]
        o = o_ref[tile, :]
        delta = delta_ref[g]
        top = jnp.full((1, TILE), HIDDEN, jnp.float32)
        total = jnp.zeros((1, TILE), jnp.float32)
        for j in range(CHUNKS):
            at = slice(j * PAIR, (j + 1) * PAIR)
            s = dot(k_s[at, :], q, NT)
            seen = row >= low - j * PAIR
            if (j + 1) * PAIR > WINDOW:
                seen = seen & (row <= high - j * PAIR)
            s = jnp.where(seen, s, HIDDEN)
            peak = jnp.maximum(top, jnp.max(s, 0, keepdims=True))
            p = jnp.exp2((s - peak) * RATE)
            p_s[at, :] = p
            m_s[j] = peak
            total = total * jnp.exp2((top - peak) * RATE) + jnp.sum(p, 0, keepdims=True)
            top = peak
        share = 1.0 / total
        for j in range(CHUNKS):
            at = slice(j * PAIR, (j + 1) * PAIR)
            p = p_s[at, :] * (jnp.exp2((m_s[j] - top) * RATE) * share)
            dp = dot(v_s[at, :], o, NT)
            ds = (p * (dp - delta)).astype(jnp.bfloat16)
            dv_s[at, :] += dot(p.astype(jnp.bfloat16), o, NN)
            dk_s[at, :] += dot(ds, q, NN)

    def give(j, block):
        for slot, ref in enumerate((near_out, far_out)):
            core = c if slot == 0 else 1 - c
            src = pl.ds(pl.multiple_of(j * PAIR + core * ROWS, ROWS), ROWS)
            ref[block, :, :HD] = (dk_s[src, :] * SCALE).astype(jnp.bfloat16)
            ref[block, :, HD:] = dv_s[src, :].astype(jnp.bfloat16)

    @pl.loop(0, RING)
    def store(step):
        give(jnp.where(step > z, step - z, step - z + 2 * RING), 2 * step)
        give(RING + step - z, 2 * step + 1)

    give(0, 2 * RING)


def attention(place, kv, q, o, delta, doc):
    out = jax.ShapeDtypeStruct((2 * RING + 1, ROWS, 2 * HD), jnp.bfloat16)
    heads = q.shape[0] // ROWS
    vmem = pl.BlockSpec(memory_space=pltpu.VMEM)
    return pl.pallas_call(
        attend,
        out_shape=(out, out),
        in_specs=[pl.BlockSpec(memory_space=pltpu.SMEM)] + [vmem] * 10,
        out_specs=(vmem, vmem),
        scratch_shapes=[
            pltpu.VMEM((SPAN, HD), jnp.bfloat16),
            pltpu.VMEM((SPAN, HD), jnp.bfloat16),
            pltpu.VMEM((SPAN, TILE), jnp.float32),
            pltpu.VMEM((CHUNKS, 1, TILE), jnp.float32),
            pltpu.VMEM((SPAN, HD), jnp.float32),
            pltpu.VMEM((SPAN, HD), jnp.float32),
        ],
        compiler_params=pltpu.CompilerParams(vmem_limit_bytes=48 << 20),
        cost_estimate=pl.CostEstimate(
            flops=8 * heads * ROWS * SPAN * HD,
            bytes_accessed=8 << 20,
            transcendentals=heads * ROWS * SPAN,
        ),
        name="attend",
    )(place, *kv, q, o, delta, doc)


def project(core, rows_ref, own_ref, far_ref, sent, w_s):
    depth = w_s.shape[0] // (2 * RING)
    counts = jnp.zeros((8, HD), jnp.float32)
    for slot, ref in enumerate((own_ref, far_ref)):
        c = core[0] if slot == 0 else 1 - core[0]
        for i in range(RING):
            at = pl.ds(pl.multiple_of((2 * i + c) * depth, depth), depth)
            w_s[at, :HD] = ref[i, :depth, :]
            w_s[at, HD:] = ref[i, depth : 2 * depth, :]
            counts = counts + ref[i, 2 * depth :, :].astype(jnp.float32)[:8]
    rows = rows_ref[...].reshape(-1, rows_ref.shape[2])
    places = rows_ref.shape[0]
    sent[:, :ROWS, :] = dot(rows, w_s[...], NN).reshape(places, ROWS, 2 * HD)
    sent[:, ROWS:, :HD] = jnp.broadcast_to(counts[None], (places, 8, HD))
    sent[:, ROWS:, HD:] = jnp.zeros((places, 8, HD), jnp.float32)


def weight_terms(core, rows_ref, terms_ref, near, far):
    c = core[0]
    depth = near.shape[1]
    terms = terms_ref[...]
    for z in range(RING):
        cols = rows_ref[:, :, z * 2 * depth : (z + 1) * 2 * depth]
        block = dot(cols.reshape(-1, 2 * depth), terms, TN)
        lower, upper = block[:depth], block[depth:]
        near[z] = jnp.where(c == 0, lower, upper)
        far[z] = jnp.where(c == 0, upper, lower).astype(jnp.bfloat16)


def input_terms(terms_ref, w_ref, out):
    heads, width = w_ref.shape[:2]
    step = 512
    for n in range(0, width, step):
        total = dot(terms_ref[0], w_ref[0, n : n + step, :], NT)
        for h in range(1, heads):
            total = total + dot(terms_ref[h], w_ref[h, n : n + step, :], NT)
        out[:, n : n + step] = total


def kernel_call(f, out_shape, inputs, scratch=(), flops=0):
    smem, vmem = pl.BlockSpec(memory_space=pltpu.SMEM), pl.BlockSpec(memory_space=pltpu.VMEM)
    return pl.pallas_call(
        f,
        out_shape=out_shape,
        in_specs=[smem if a.ndim == 1 else vmem for a in inputs],
        out_specs=jax.tree.map(lambda _: vmem, out_shape),
        scratch_shapes=scratch,
        compiler_params=pltpu.CompilerParams(vmem_limit_bytes=40 << 20),
        cost_estimate=pl.CostEstimate(flops=flops, bytes_accessed=8 << 20, transcendentals=0),
        name=f.__name__,
    )(*inputs)


def split_columns(a, parts):
    rows, width = a.shape[0], a.shape[1] // parts

    def move(src, dst):
        dst[0] = src[...]

    return pl.pallas_call(
        move,
        grid=(parts,),
        out_shape=jax.ShapeDtypeStruct((parts, rows, width), a.dtype),
        in_specs=[pl.BlockSpec((rows, width), lambda i: (0, i))],
        out_specs=pl.BlockSpec((1, rows, width), lambda i: (i, 0, 0)),
        name="split_columns",
    )(a)


def swap(a, axis="c"):
    return lax.ppermute(a, axis, [(0, 1), (1, 0)])


def body(tokens_in, w_key, w_value, queries, out_grad, attn_out, doc_ids):
    f32, bf16 = jnp.float32, jnp.bfloat16
    heads = queries.shape[1] // HD
    y, zb, za, c = (lax.axis_index(name) for name in ("y", "zb", "za", "c"))
    z = zb * 2 + za
    ys = lax.axis_size("y")
    xs = lax.axis_size("x")
    depth = w_key.shape[0]
    model = tokens_in.shape[1]
    shape = jax.ShapeDtypeStruct
    core = c.astype(jnp.int32)[None]
    place = jnp.stack([z, c, za]).astype(jnp.int32)

    cut = split_columns(tokens_in, ys)
    rows_y = lax.all_to_all(cut, "y", 0, 0)

    turned = lax.ppermute(
        jnp.concatenate((w_key, w_value), 1),
        ("y", "x"),
        [(a * xs + b, b * xs + a) for a in range(ys) for b in range(xs)],
    )

    before = jnp.stack([jnp.sum(doc_ids < 1), jnp.sum(doc_ids < 2)]).astype(f32)
    counts = jnp.zeros((16, HD), f32).at[0, :2].set(before).astype(bf16)
    w_own = lax.all_gather(
        jnp.concatenate((w_key, w_value, counts), 0), ("zb", "za"), axis=0
    )
    w_far = swap(w_own)

    def by_head(a):
        return a.reshape(ROWS, heads, HD).swapaxes(0, 1)

    delta = jnp.sum(
        out_grad.astype(f32).reshape(ROWS, heads, HD)
        * attn_out.astype(f32).reshape(ROWS, heads, HD),
        -1,
    )
    delta = delta.T.reshape(heads // GROUP, 1, TILE)
    doc_tile = jnp.tile(doc_ids, GROUP)[None]
    q_rows = by_head(queries).reshape(heads * ROWS, HD)
    o_rows = by_head(out_grad).reshape(heads * ROWS, HD)

    quarter = model // ys
    sent = kernel_call(
        project,
        shape((ys, ROWS + 8, 2 * HD), f32),
        (core, rows_y, w_own, w_far),
        [pltpu.VMEM((quarter, 2 * HD), bf16)],
        2 * ys * ROWS * quarter * 2 * HD,
    )
    got = lax.all_to_all(sent, "y", 0, 0)
    kv = jnp.sum(got[:, :ROWS], 0).astype(bf16)
    starts = jnp.sum(got[:, ROWS], 0)

    origin = (y * RING + z - WINDOW // PAIR) * PAIR
    starts = jnp.concatenate((jnp.zeros((1,), jnp.int32), starts[:2].astype(jnp.int32)))
    window = jnp.concatenate((place, starts - origin))

    turned, _ = lax.optimization_barrier((turned, kv))
    w_all = lax.all_gather(turned, ("y", "zb", "za", "c"), axis=0, tiled=True)
    w_all = w_all.reshape(xs, quarter, 2 * HD)

    pair = jnp.concatenate((kv, swap(kv, "za")), 0)
    own2 = lax.all_gather(pair, "zb", axis=0, tiled=True)
    own1 = lax.ppermute(own2, "y", [(i, i + 1) for i in range(ys - 1)])
    own0 = lax.ppermute(own2, "y", [(i, i + 2) for i in range(ys - 2)])
    far2, far1, far0 = swap(own2), swap(own1), swap(own0)

    near, far = attention(
        window, (own0, own1, own2, far0, far1, far2), q_rows, o_rows, delta, doc_tile
    )

    mine = (near.astype(f32) + swap(far).astype(f32)).astype(bf16)
    ring = ("zb", "za")
    parts = lax.all_to_all(mine[:-1].reshape(RING, 2, ROWS, 2 * HD), ring, 0, 0)
    parts = parts.astype(f32)
    here = (jnp.arange(RING) >= z).astype(f32)[:, None, None]
    back = (jnp.sum((1 - here) * parts[:, 0], 0) + mine[-1].astype(f32)).astype(bf16)
    back = jnp.stack((jnp.sum(here * parts[:, 0], 0), jnp.sum(parts[:, 1], 0))).astype(bf16), back[None]
    sums = lax.all_gather(jnp.concatenate(back), "y", axis=0).astype(f32)
    sums = jnp.pad(sums, ((0, 2), (0, 0), (0, 0), (0, 0)))
    terms_y = (sums[:ys, 0] + sums[1 : ys + 1, 1] + sums[2 : ys + 2, 2]).astype(bf16)
    grad_terms = lax.dynamic_index_in_dim(terms_y, y, 0, keepdims=False)

    terms_y = terms_y.reshape(ys * ROWS, 2 * HD)
    dims = (RING, depth, 2 * HD)
    near, far = kernel_call(
        weight_terms,
        (shape(dims, f32), shape(dims, bf16)),
        (core, rows_y, terms_y),
        (),
        2 * ys * ROWS * quarter * 2 * HD,
    )
    summed = (near + swap(far).astype(f32)).astype(bf16)
    parts = lax.all_to_all(summed, ring, 0, 0)

    terms_x = lax.all_gather(grad_terms, "x", axis=0)
    input_grad = kernel_call(
        input_terms,
        shape((ROWS, quarter), f32),
        (terms_x, w_all),
        (),
        2 * ROWS * quarter * xs * 2 * HD,
    )
    parts, input_grad = lax.optimization_barrier((parts, input_grad))
    grads = jnp.sum(parts.astype(f32), 0)
    return (grads[:, :HD], grads[:, HD:], input_grad)


def solution(mesh):
    fine = Mesh(
        mesh.devices.reshape(4, RING // 2, 2, 2, 4), ("y", "zb", "za", "c", "x")
    )
    ctx = ("y", "zb", "za", "c")
    split = P(ctx, "x")
    return jax.shard_map(
        body,
        mesh=fine,
        in_specs=(P(ctx, None), split, split, split, split, split, P(ctx)),
        out_specs=(split, split, split),
        check_vma=False,
    )
```

```python
import math

import jax
import jax.numpy as jnp
from jax import lax
from jax.experimental import pallas as pl
from jax.experimental.pallas import tpu as pltpu
from jax.sharding import Mesh
from jax.sharding import PartitionSpec as P

HD = 128
WINDOW = 4096
ROWS = 128
PAIR = 2 * ROWS
RING = 8
CHUNKS = WINDOW // PAIR + 1
SPAN = CHUNKS * PAIR
GROUP = 4
TILE = GROUP * ROWS
SCALE = 1.0 / math.sqrt(HD)
RATE = SCALE * math.log2(math.e)
HIDDEN = -1e30

NT = (((1,), (1,)), ((), ()))
NN = (((1,), (0,)), ((), ()))
TN = (((0,), (0,)), ((), ()))


def dot(a, b, dims):
    return lax.dot_general(a, b, dims, preferred_element_type=jnp.float32)


def attend(
    place, own, far, own_back, far_back, q_ref, o_ref, a_ref, doc_ref,
    near_out, far_out, near_back, far_out_back, k_s, v_s, p_s, m_s, dk_s, dv_s,
):
    z = place[0]
    c = place[1]

    def rows(j, slot):
        core = c if slot == 0 else 1 - c
        return pl.ds(pl.multiple_of(j * PAIR + core * ROWS, ROWS), ROWS)

    def merged(step):
        return jnp.where(step > z, step - z, step - z + 2 * RING)

    def take(j, slot, block):
        k_s[rows(j, slot), :] = block[:, :HD]
        v_s[rows(j, slot), :] = block[:, HD:]

    @pl.loop(0, RING)
    def load(step):
        for slot, ref in enumerate((own, far)):
            take(merged(step), slot, ref[step, 0])
            take(RING + step - z, slot, ref[step, 1])

    take(0, 0, own_back[...])
    take(0, 1, far_back[...])

    doc = doc_ref[...]
    token = c * ROWS + lax.broadcasted_iota(jnp.int32, (1, TILE), 1) % ROWS
    high = token + WINDOW
    start = jnp.where(doc == 0, place[2], jnp.where(doc == 1, place[3], place[4]))
    low = jnp.maximum(start, token + 1)
    row = lax.broadcasted_iota(jnp.int32, (PAIR, TILE), 0)
    dk_s[...] = jnp.zeros_like(dk_s)
    dv_s[...] = jnp.zeros_like(dv_s)

    @pl.loop(0, q_ref.shape[1] // TILE)
    def heads(g):
        def by_head(ref):
            at = [pl.ds(pl.multiple_of(g * TILE + h * HD, HD), HD) for h in range(GROUP)]
            return [ref[:, one] for one in at]

        q = jnp.concatenate(by_head(q_ref), 0)
        o_heads = by_head(o_ref)
        o = jnp.concatenate(o_heads, 0)
        products = [
            one.astype(jnp.float32) * two.astype(jnp.float32)
            for one, two in zip(o_heads, by_head(a_ref))
        ]
        delta = jnp.concatenate([jnp.sum(p.T, 0, keepdims=True) for p in products], 1)
        top = jnp.full((1, TILE), HIDDEN, jnp.float32)
        total = jnp.zeros((1, TILE), jnp.float32)
        for j in range(CHUNKS):
            at = slice(j * PAIR, (j + 1) * PAIR)
            s = dot(k_s[at, :], q, NT)
            seen = row >= low - j * PAIR
            if (j + 1) * PAIR > WINDOW:
                seen = seen & (row <= high - j * PAIR)
            s = jnp.where(seen, s, HIDDEN)
            peak = jnp.maximum(top, jnp.max(s, 0, keepdims=True))
            p = jnp.exp2((s - peak) * RATE)
            p_s[at, :] = p
            m_s[j] = peak
            total = total * jnp.exp2((top - peak) * RATE) + jnp.sum(p, 0, keepdims=True)
            top = peak
        share = 1.0 / total
        for j in range(CHUNKS):
            at = slice(j * PAIR, (j + 1) * PAIR)
            p = p_s[at, :] * (jnp.exp2((m_s[j] - top) * RATE) * share)
            dp = dot(v_s[at, :], o, NT)
            ds = (p * (dp - delta)).astype(jnp.bfloat16)
            dv_s[at, :] += dot(p.astype(jnp.bfloat16), o, NN)
            dk_s[at, :] += dot(ds, q, NN)

    def give(j, slot):
        src = rows(j, slot)
        dk = (dk_s[src, :] * SCALE).astype(jnp.bfloat16)
        return jnp.concatenate((dk, dv_s[src, :].astype(jnp.bfloat16)), 1)

    @pl.loop(0, RING)
    def store(step):
        for slot, ref in enumerate((near_out, far_out)):
            ref[step, 0] = give(merged(step), slot)
            ref[step, 1] = give(RING + step - z, slot)

    near_back[...] = give(0, 0)
    far_out_back[...] = give(0, 1)


def attention(place, kv, q, o, a, doc):
    out = jax.ShapeDtypeStruct((RING, 2, ROWS, 2 * HD), jnp.bfloat16)
    back = jax.ShapeDtypeStruct((ROWS, 2 * HD), jnp.bfloat16)
    heads = q.shape[1] // HD
    vmem = pl.BlockSpec(memory_space=pltpu.VMEM)
    return pl.pallas_call(
        attend,
        out_shape=(out, out, back, back),
        in_specs=[pl.BlockSpec(memory_space=pltpu.SMEM)] + [vmem] * 8,
        out_specs=(vmem,) * 4,
        scratch_shapes=[
            pltpu.VMEM((SPAN, HD), jnp.bfloat16),
            pltpu.VMEM((SPAN, HD), jnp.bfloat16),
            pltpu.VMEM((SPAN, TILE), jnp.float32),
            pltpu.VMEM((CHUNKS, 1, TILE), jnp.float32),
            pltpu.VMEM((SPAN, HD), jnp.float32),
            pltpu.VMEM((SPAN, HD), jnp.float32),
        ],
        compiler_params=pltpu.CompilerParams(vmem_limit_bytes=48 << 20),
        cost_estimate=pl.CostEstimate(
            flops=8 * heads * ROWS * SPAN * HD,
            bytes_accessed=8 << 20,
            transcendentals=heads * ROWS * SPAN,
        ),
        name="attend",
    )(place, *kv, q, o, a, doc)


def project(core, rows_ref, own_ref, far_ref, sent, w_s):
    depth = w_s.shape[0] // (2 * RING)
    counts = jnp.zeros((8, HD), jnp.float32)
    for slot, ref in enumerate((own_ref, far_ref)):
        c = core[0] if slot == 0 else 1 - core[0]
        for i in range(RING):
            at = pl.ds(pl.multiple_of((2 * i + c) * depth, depth), depth)
            w_s[at, :HD] = ref[i, :depth, :]
            w_s[at, HD:] = ref[i, depth : 2 * depth, :]
            counts = counts + ref[i, 2 * depth :, :].astype(jnp.float32)[:8]
    rows = rows_ref[...].reshape(-1, rows_ref.shape[2])
    places = rows_ref.shape[0]
    sent[:, :ROWS, :] = dot(rows, w_s[...], NN).reshape(places, ROWS, 2 * HD)
    sent[:, ROWS:, :HD] = jnp.broadcast_to(counts[None], (places, 8, HD))
    sent[:, ROWS:, HD:] = jnp.zeros((places, 8, HD), jnp.float32)


def window_sums(place, parts_ref, back_ref, out):
    same = jnp.zeros((ROWS, 2 * HD), jnp.float32)
    after = same
    last = back_ref[...]
    for step in range(RING):
        block = parts_ref[step, 0].astype(jnp.float32)
        mine = step >= place[0]
        same = same + jnp.where(mine, block, 0.0)
        last = last + jnp.where(mine, 0.0, block)
        after = after + parts_ref[step, 1].astype(jnp.float32)
    for i, total in enumerate((same, after, last)):
        out[i] = total.astype(jnp.bfloat16)


def weight_terms(place, rows_ref, sums_ref, near, far, own_terms):
    c = place[0]
    depth = near.shape[1]
    places = sums_ref.shape[0]
    blocks = []
    for i in range(places):
        total = sums_ref[i, 0].astype(jnp.float32)
        for k in range(1, min(3, places - i)):
            total = total + sums_ref[i + k, k].astype(jnp.float32)
        blocks.append(total.astype(jnp.bfloat16))

        @pl.when(place[1] == i)
        def _(block=blocks[i]):
            own_terms[...] = block

    terms = jnp.concatenate(blocks, 0)
    for z in range(RING):
        cols = rows_ref[:, :, z * 2 * depth : (z + 1) * 2 * depth]
        block = dot(cols.reshape(-1, 2 * depth), terms, TN)
        lower, upper = block[:depth], block[depth:]
        near[z] = jnp.where(c == 0, lower, upper)
        far[z] = jnp.where(c == 0, upper, lower).astype(jnp.bfloat16)


def input_terms(place, terms_ref, *refs):
    w_refs, out = refs[:-1], refs[-1]
    pieces = len(w_refs) // 2
    heads = terms_ref.shape[0]
    depth = w_refs[0].shape[1]
    even = place[0] == 0
    for z in range(RING):
        total = jnp.zeros((ROWS, 2 * depth), jnp.float32)
        for k in range(heads):
            upper = z // (RING // 2)
            at = k if k < 2 else (2 + upper if k == 2 else k + 1)
            block = z % (RING // 2) if k == 2 else z
            own, far = w_refs[at][block], w_refs[pieces + at][block]
            w = jnp.concatenate((jnp.where(even, own, far), jnp.where(even, far, own)), 0)
            total = total + dot(terms_ref[(place[1] + heads - k) % heads], w, NT)
        out[:, 2 * z * depth : 2 * (z + 1) * depth] = total


def kernel_call(f, out_shape, inputs, scratch=(), flops=0):
    smem, vmem = pl.BlockSpec(memory_space=pltpu.SMEM), pl.BlockSpec(memory_space=pltpu.VMEM)
    return pl.pallas_call(
        f,
        out_shape=out_shape,
        in_specs=[smem if a.ndim == 1 else vmem for a in inputs],
        out_specs=jax.tree.map(lambda _: vmem, out_shape),
        scratch_shapes=scratch,
        compiler_params=pltpu.CompilerParams(vmem_limit_bytes=40 << 20),
        cost_estimate=pl.CostEstimate(flops=flops, bytes_accessed=8 << 20, transcendentals=0),
        name=f.__name__,
    )(*inputs)


def split_columns(a, parts):
    rows, width = a.shape[0], a.shape[1] // parts

    def move(src, dst):
        dst[0] = src[...]

    return pl.pallas_call(
        move,
        grid=(parts,),
        out_shape=jax.ShapeDtypeStruct((parts, rows, width), a.dtype),
        in_specs=[pl.BlockSpec((rows, width), lambda i: (0, i))],
        out_specs=pl.BlockSpec((1, rows, width), lambda i: (i, 0, 0)),
        name="split_columns",
    )(a)


def swap(a, axis="c"):
    return lax.ppermute(a, axis, [(0, 1), (1, 0)])


def body(tokens_in, w_key, w_value, queries, out_grad, attn_out, doc_ids):
    f32, bf16 = jnp.float32, jnp.bfloat16
    y, zb, za, c = (lax.axis_index(name) for name in ("y", "zb", "za", "c"))
    z = zb * 2 + za
    ys = lax.axis_size("y")
    xs = lax.axis_size("x")
    depth = w_key.shape[0]
    model = tokens_in.shape[1]
    shape = jax.ShapeDtypeStruct
    core = c.astype(jnp.int32)[None]
    place = jnp.stack([z, c]).astype(jnp.int32)

    cut = split_columns(tokens_in, ys)
    rows_y = lax.all_to_all(cut, "y", 0, 0)

    turned = lax.ppermute(
        jnp.concatenate((w_key, w_value), 1),
        ("y", "x"),
        [(a * xs + b, b * xs + a) for a in range(ys) for b in range(xs)],
    )

    before = jnp.stack([jnp.sum(doc_ids < 1), jnp.sum(doc_ids < 2)]).astype(f32)
    counts = jnp.zeros((16, HD), f32).at[0, :2].set(before).astype(bf16)
    w_near = lax.all_gather(
        jnp.concatenate((w_key, w_value, counts), 0), ("zb", "za"), axis=0
    )
    w_other = swap(w_near)

    doc_tile = jnp.tile(doc_ids, GROUP)[None]

    quarter = model // ys
    sent = kernel_call(
        project,
        shape((ys, ROWS + 8, 2 * HD), f32),
        (core, rows_y, w_near, w_other),
        [pltpu.VMEM((quarter, 2 * HD), bf16)],
        2 * ys * ROWS * quarter * 2 * HD,
    )
    got = lax.all_to_all(sent, "y", 0, 0)
    kv = jnp.sum(got[:, :ROWS], 0).astype(bf16)
    starts = jnp.sum(got[:, ROWS], 0)

    origin = (y * RING + z - WINDOW // PAIR) * PAIR
    starts = jnp.concatenate((jnp.zeros((1,), jnp.int32), starts[:2].astype(jnp.int32)))
    window = jnp.concatenate((place, starts - origin))

    ring = ("zb", "za")
    before1 = lax.ppermute(kv, "y", [(i, i + 1) for i in range(ys - 1)])
    before2 = lax.ppermute(kv, "y", [(i, i + 2) for i in range(ys - 2)])
    onward = (jnp.arange(RING) >= z)[:, None, None]
    send = jnp.stack(
        (
            jnp.where(onward, kv[None], before2[None]),
            jnp.broadcast_to(before1[None], (RING, ROWS, 2 * HD)),
        ),
        1,
    )
    own = lax.all_to_all(send, ring, 0, 0)

    turned, own = lax.optimization_barrier((turned, own))
    w_z = lax.all_to_all(jnp.broadcast_to(turned[None], (RING, *turned.shape)), ring, 0, 0)

    near, far, near_back, far_back = attention(
        window, (own, swap(own), before2, swap(before2)), queries, out_grad, attn_out, doc_tile
    )

    mine = (near.astype(f32) + swap(far).astype(f32)).astype(bf16)
    mine_back = near_back.astype(f32) + swap(far_back).astype(f32)
    w_z, mine = lax.optimization_barrier((w_z, mine))
    parts = lax.all_to_all(mine, ring, 0, 0)

    def along(a, k):
        return lax.ppermute(a, "y", [(i, (i + k) % ys) for i in range(ys)])

    w_1, w_3 = along(w_z, 1), along(w_z, 3)
    half = RING // 2
    w_2 = along(w_1[:half], 1), along(w_3[half:], 3)
    parts, w_z, w_1, w_3, *w_2 = lax.optimization_barrier((parts, w_z, w_1, w_3, *w_2))
    w_own = [w_z, w_1, *w_2, w_3]
    w_far = [swap(one) for one in w_own]
    sums = kernel_call(
        window_sums,
        shape((3, ROWS, 2 * HD), bf16),
        (place, parts, mine_back),
    )
    sums = lax.all_gather(sums, "y", axis=0)

    dims = (RING, depth, 2 * HD)
    near, far, grad_terms = kernel_call(
        weight_terms,
        (shape(dims, f32), shape(dims, bf16), shape((ROWS, 2 * HD), bf16)),
        (jnp.stack([c, y]).astype(jnp.int32), rows_y, sums),
        (),
        2 * ys * ROWS * quarter * 2 * HD,
    )
    summed = (near + swap(far).astype(f32)).astype(bf16)
    parts = lax.all_to_all(summed, ring, 0, 0)

    tied, *w_far = lax.optimization_barrier((grad_terms, *w_far))
    terms_x = lax.all_gather(tied, "x", axis=0)
    input_grad = kernel_call(
        input_terms,
        shape((ROWS, quarter), f32),
        (jnp.stack([c, y]).astype(jnp.int32), terms_x, *w_own, *w_far),
        (),
        2 * ROWS * quarter * xs * 2 * HD,
    )
    parts, input_grad = lax.optimization_barrier((parts, input_grad))
    grads = jnp.sum(parts.astype(f32), 0)
    return (grads[:, :HD], grads[:, HD:], input_grad)


def solution(mesh):
    fine = Mesh(
        mesh.devices.reshape(4, RING // 2, 2, 2, 4), ("y", "zb", "za", "c", "x")
    )
    ctx = ("y", "zb", "za", "c")
    split = P(ctx, "x")
    return jax.shard_map(
        body,
        mesh=fine,
        in_specs=(P(ctx, None), split, split, split, split, split, P(ctx)),
        out_specs=(split, split, split),
        check_vma=False,
    )
```

```python
import math

import jax
import jax.numpy as jnp
from jax import lax
from jax.experimental import pallas as pl
from jax.experimental.pallas import tpu as pltpu
from jax.sharding import Mesh
from jax.sharding import PartitionSpec as P

HD = 128
WINDOW = 4096
ROWS = 128
PAIR = 2 * ROWS
RING = 8
CHUNKS = WINDOW // PAIR + 1
SPAN = CHUNKS * PAIR
GROUP = 4
TILE = GROUP * ROWS
SCALE = 1.0 / math.sqrt(HD)
RATE = SCALE * math.log2(math.e)
HIDDEN = -1e30

NT = (((1,), (1,)), ((), ()))
NN = (((1,), (0,)), ((), ()))
TN = (((0,), (0,)), ((), ()))


def dot(a, b, dims):
    return lax.dot_general(a, b, dims, preferred_element_type=jnp.float32)


def attend(
    place, own, far, own_back, far_back, q_ref, o_ref, a_ref, doc_ref,
    near_out, far_out, near_back, far_out_back, k_s, v_s, p_s, m_s, dk_s, dv_s,
):
    z = place[0]
    c = place[1]

    def rows(j, slot):
        core = c if slot == 0 else 1 - c
        return pl.ds(pl.multiple_of(j * PAIR + core * ROWS, ROWS), ROWS)

    def merged(step):
        return jnp.where(step > z, step - z, step - z + 2 * RING)

    def take(j, slot, block):
        k_s[rows(j, slot), :] = block[:, :HD]
        v_s[rows(j, slot), :] = block[:, HD:]

    @pl.loop(0, RING)
    def load(step):
        for slot, ref in enumerate((own, far)):
            take(merged(step), slot, ref[step, 0])
            take(RING + step - z, slot, ref[step, 1])

    take(0, 0, own_back[...])
    take(0, 1, far_back[...])

    doc = doc_ref[...]
    token = c * ROWS + lax.broadcasted_iota(jnp.int32, (1, TILE), 1) % ROWS
    high = token + WINDOW
    start = jnp.where(doc == 0, place[2], jnp.where(doc == 1, place[3], place[4]))
    low = jnp.maximum(start, token + 1)
    row = lax.broadcasted_iota(jnp.int32, (PAIR, TILE), 0)
    dk_s[...] = jnp.zeros_like(dk_s)
    dv_s[...] = jnp.zeros_like(dv_s)

    @pl.loop(0, q_ref.shape[1] // TILE)
    def heads(g):
        def by_head(ref):
            at = [pl.ds(pl.multiple_of(g * TILE + h * HD, HD), HD) for h in range(GROUP)]
            return [ref[:, one] for one in at]

        q = jnp.concatenate(by_head(q_ref), 0)
        o_heads = by_head(o_ref)
        o = jnp.concatenate(o_heads, 0)
        products = [
            one.astype(jnp.float32) * two.astype(jnp.float32)
            for one, two in zip(o_heads, by_head(a_ref))
        ]
        delta = jnp.concatenate([jnp.sum(p.T, 0, keepdims=True) for p in products], 1)
        top = jnp.full((1, TILE), HIDDEN, jnp.float32)
        total = jnp.zeros((1, TILE), jnp.float32)
        for j in range(CHUNKS):
            at = slice(j * PAIR, (j + 1) * PAIR)
            s = dot(k_s[at, :], q, NT)
            seen = row >= low - j * PAIR
            if (j + 1) * PAIR > WINDOW:
                seen = seen & (row <= high - j * PAIR)
            s = jnp.where(seen, s, HIDDEN)
            peak = jnp.maximum(top, jnp.max(s, 0, keepdims=True))
            p = jnp.exp2((s - peak) * RATE)
            p_s[at, :] = p
            m_s[j] = peak
            total = total * jnp.exp2((top - peak) * RATE) + jnp.sum(p, 0, keepdims=True)
            top = peak
        share = 1.0 / total
        for j in range(CHUNKS):
            at = slice(j * PAIR, (j + 1) * PAIR)
            p = p_s[at, :] * (jnp.exp2((m_s[j] - top) * RATE) * share)
            dp = dot(v_s[at, :], o, NT)
            ds = (p * (dp - delta)).astype(jnp.bfloat16)
            dv_s[at, :] += dot(p.astype(jnp.bfloat16), o, NN)
            dk_s[at, :] += dot(ds, q, NN)

    def give(j, slot):
        src = rows(j, slot)
        dk = (dk_s[src, :] * SCALE).astype(jnp.bfloat16)
        return jnp.concatenate((dk, dv_s[src, :].astype(jnp.bfloat16)), 1)

    @pl.loop(0, RING)
    def store(step):
        for slot, ref in enumerate((near_out, far_out)):
            ref[step, 0] = give(merged(step), slot)
            ref[step, 1] = give(RING + step - z, slot)

    near_back[...] = give(0, 0)
    far_out_back[...] = give(0, 1)


def attention(place, kv, q, o, a, doc):
    out = jax.ShapeDtypeStruct((RING, 2, ROWS, 2 * HD), jnp.bfloat16)
    back = jax.ShapeDtypeStruct((ROWS, 2 * HD), jnp.bfloat16)
    heads = q.shape[1] // HD
    vmem = pl.BlockSpec(memory_space=pltpu.VMEM)
    return pl.pallas_call(
        attend,
        out_shape=(out, out, back, back),
        in_specs=[pl.BlockSpec(memory_space=pltpu.SMEM)] + [vmem] * 8,
        out_specs=(vmem,) * 4,
        scratch_shapes=[
            pltpu.VMEM((SPAN, HD), jnp.bfloat16),
            pltpu.VMEM((SPAN, HD), jnp.bfloat16),
            pltpu.VMEM((SPAN, TILE), jnp.float32),
            pltpu.VMEM((CHUNKS, 1, TILE), jnp.float32),
            pltpu.VMEM((SPAN, HD), jnp.float32),
            pltpu.VMEM((SPAN, HD), jnp.float32),
        ],
        compiler_params=pltpu.CompilerParams(vmem_limit_bytes=48 << 20),
        cost_estimate=pl.CostEstimate(
            flops=8 * heads * ROWS * SPAN * HD,
            bytes_accessed=8 << 20,
            transcendentals=heads * ROWS * SPAN,
        ),
        name="attend",
    )(place, *kv, q, o, a, doc)


def project(core, rows_ref, own_ref, far_ref, sent, w_s):
    depth = w_s.shape[0] // (2 * RING)
    counts = jnp.zeros((8, HD), jnp.float32)
    for slot, ref in enumerate((own_ref, far_ref)):
        c = core[0] if slot == 0 else 1 - core[0]
        for i in range(RING):
            at = pl.ds(pl.multiple_of((2 * i + c) * depth, depth), depth)
            w_s[at, :HD] = ref[i, :depth, :]
            w_s[at, HD:] = ref[i, depth : 2 * depth, :]
            counts = counts + ref[i, 2 * depth :, :].astype(jnp.float32)[:8]
    rows = rows_ref[...].reshape(-1, rows_ref.shape[2])
    places = rows_ref.shape[0]
    sent[:, :ROWS, :] = dot(rows, w_s[...], NN).reshape(places, ROWS, 2 * HD)
    sent[:, ROWS:, :HD] = jnp.broadcast_to(counts[None], (places, 8, HD))
    sent[:, ROWS:, HD:] = jnp.zeros((places, 8, HD), jnp.float32)


def window_sums(place, parts_ref, back_ref, out):
    same = jnp.zeros((ROWS, 2 * HD), jnp.float32)
    after = same
    last = back_ref[...]
    for step in range(RING):
        block = parts_ref[step, 0].astype(jnp.float32)
        mine = step >= place[0]
        same = same + jnp.where(mine, block, 0.0)
        last = last + jnp.where(mine, 0.0, block)
        after = after + parts_ref[step, 1].astype(jnp.float32)
    for i, total in enumerate((same, after, last)):
        out[i] = total.astype(jnp.bfloat16)


def weight_terms(place, rows_ref, sums_ref, near, far, own_terms):
    c = place[0]
    depth = near.shape[1]
    places = sums_ref.shape[0]
    blocks = []
    for i in range(places):
        total = sums_ref[i, 0].astype(jnp.float32)
        for k in range(1, min(3, places - i)):
            total = total + sums_ref[i + k, k].astype(jnp.float32)
        blocks.append(total.astype(jnp.bfloat16))

        @pl.when(place[1] == i)
        def _(block=blocks[i]):
            own_terms[...] = block

    terms = jnp.concatenate(blocks, 0)
    for z in range(RING):
        cols = rows_ref[:, :, z * 2 * depth : (z + 1) * 2 * depth]
        block = dot(cols.reshape(-1, 2 * depth), terms, TN)
        lower, upper = block[:depth], block[depth:]
        near[z] = jnp.where(c == 0, lower, upper)
        far[z] = jnp.where(c == 0, upper, lower).astype(jnp.bfloat16)


def input_terms(place, terms_ref, *refs):
    w_refs, out = refs[:-1], refs[-1]
    pieces = len(w_refs) // 2
    heads = terms_ref.shape[0]
    depth = w_refs[0].shape[1]
    even = place[0] == 0
    for z in range(RING):
        total = jnp.zeros((ROWS, 2 * depth), jnp.float32)
        for k in range(heads):
            upper = z // (RING // 2)
            at = k if k < 2 else (2 + upper if k == 2 else k + 1)
            block = z % (RING // 2) if k == 2 else z
            own, far = w_refs[at][block], w_refs[pieces + at][block]
            w = jnp.concatenate((jnp.where(even, own, far), jnp.where(even, far, own)), 0)
            total = total + dot(terms_ref[(place[1] + heads - k) % heads], w, NT)
        out[:, 2 * z * depth : 2 * (z + 1) * depth] = total


def kernel_call(f, out_shape, inputs, scratch=(), flops=0):
    smem, vmem = pl.BlockSpec(memory_space=pltpu.SMEM), pl.BlockSpec(memory_space=pltpu.VMEM)
    return pl.pallas_call(
        f,
        out_shape=out_shape,
        in_specs=[smem if a.ndim == 1 else vmem for a in inputs],
        out_specs=jax.tree.map(lambda _: vmem, out_shape),
        scratch_shapes=scratch,
        compiler_params=pltpu.CompilerParams(vmem_limit_bytes=40 << 20),
        cost_estimate=pl.CostEstimate(flops=flops, bytes_accessed=8 << 20, transcendentals=0),
        name=f.__name__,
    )(*inputs)


def split_columns(a, parts):
    rows, width = a.shape[0], a.shape[1] // parts

    def move(src, dst):
        dst[0] = src[...]

    return pl.pallas_call(
        move,
        grid=(parts,),
        out_shape=jax.ShapeDtypeStruct((parts, rows, width), a.dtype),
        in_specs=[pl.BlockSpec((rows, width), lambda i: (0, i))],
        out_specs=pl.BlockSpec((1, rows, width), lambda i: (i, 0, 0)),
        name="split_columns",
    )(a)


def swap(a, axis="c"):
    return lax.ppermute(a, axis, [(0, 1), (1, 0)])


def body(tokens_in, w_key, w_value, queries, out_grad, attn_out, doc_ids):
    f32, bf16 = jnp.float32, jnp.bfloat16
    y, zb, za, c = (lax.axis_index(name) for name in ("y", "zb", "za", "c"))
    z = zb * 2 + za
    ys = lax.axis_size("y")
    xs = lax.axis_size("x")
    depth = w_key.shape[0]
    model = tokens_in.shape[1]
    shape = jax.ShapeDtypeStruct
    core = c.astype(jnp.int32)[None]
    place = jnp.stack([z, c]).astype(jnp.int32)

    cut = split_columns(tokens_in, ys)
    rows_y = lax.all_to_all(cut, "y", 0, 0)

    turned = lax.ppermute(
        jnp.concatenate((w_key, w_value), 1),
        ("y", "x"),
        [(a * xs + b, b * xs + a) for a in range(ys) for b in range(xs)],
    )

    before = jnp.stack([jnp.sum(doc_ids < 1), jnp.sum(doc_ids < 2)]).astype(f32)
    counts = jnp.zeros((16, HD), f32).at[0, :2].set(before).astype(bf16)
    w_near = lax.all_gather(
        jnp.concatenate((w_key, w_value, counts), 0), ("zb", "za"), axis=0
    )
    w_other = swap(w_near)

    doc_tile = jnp.tile(doc_ids, GROUP)[None]

    quarter = model // ys
    sent = kernel_call(
        project,
        shape((ys, ROWS + 8, 2 * HD), f32),
        (core, rows_y, w_near, w_other),
        [pltpu.VMEM((quarter, 2 * HD), bf16)],
        2 * ys * ROWS * quarter * 2 * HD,
    )
    got = lax.all_to_all(sent, "y", 0, 0)
    kv = jnp.sum(got[:, :ROWS], 0).astype(bf16)
    starts = jnp.sum(got[:, ROWS], 0)

    origin = (y * RING + z - WINDOW // PAIR) * PAIR
    starts = jnp.concatenate((jnp.zeros((1,), jnp.int32), starts[:2].astype(jnp.int32)))
    window = jnp.concatenate((place, starts - origin))

    ring = ("zb", "za")
    before1 = lax.ppermute(kv, "y", [(i, i + 1) for i in range(ys - 1)])
    before2 = lax.ppermute(kv, "y", [(i, i + 2) for i in range(ys - 2)])
    onward = (jnp.arange(RING) >= z)[:, None, None]
    send = jnp.stack(
        (
            jnp.where(onward, kv[None], before2[None]),
            jnp.broadcast_to(before1[None], (RING, ROWS, 2 * HD)),
        ),
        1,
    )
    own = lax.all_to_all(send, ring, 0, 0)

    turned, own = lax.optimization_barrier((turned, own))
    w_z = lax.all_to_all(jnp.broadcast_to(turned[None], (RING, *turned.shape)), ring, 0, 0)

    near, far, near_back, far_back = attention(
        window, (own, swap(own), before2, swap(before2)), queries, out_grad, attn_out, doc_tile
    )

    mine = (near.astype(f32) + swap(far).astype(f32)).astype(bf16)
    mine_back = near_back.astype(f32) + swap(far_back).astype(f32)
    w_z, mine = lax.optimization_barrier((w_z, mine))
    parts = lax.all_to_all(mine, ring, 0, 0)

    def along(a, k):
        return lax.ppermute(a, "y", [(i, (i + k) % ys) for i in range(ys)])

    w_1, w_3 = along(w_z, 1), along(w_z, 3)
    parts, w_z, w_1, w_3 = lax.optimization_barrier((parts, w_z, w_1, w_3))
    half = RING // 2
    w_2 = along(w_1[:half], 1), along(w_3[half:], 3)
    f_z, f_1, f_3 = swap(w_z), swap(w_1), swap(w_3)
    sums = kernel_call(
        window_sums,
        shape((3, ROWS, 2 * HD), bf16),
        (place, parts, mine_back),
    )
    sums = lax.all_gather(sums, "y", axis=0)
    sums, *w_2 = lax.optimization_barrier((sums, *w_2))

    dims = (RING, depth, 2 * HD)
    near, far, grad_terms = kernel_call(
        weight_terms,
        (shape(dims, f32), shape(dims, bf16), shape((ROWS, 2 * HD), bf16)),
        (jnp.stack([c, y]).astype(jnp.int32), rows_y, sums),
        (),
        2 * ys * ROWS * quarter * 2 * HD,
    )
    summed = (near + swap(far).astype(f32)).astype(bf16)
    parts = lax.all_to_all(summed, ring, 0, 0)

    w_far = [f_z, f_1, *(swap(one) for one in w_2), f_3]
    tied, *w_far = lax.optimization_barrier((grad_terms, *w_far))
    w_own = [w_z, w_1, *w_2, w_3]
    terms_x = lax.all_gather(tied, "x", axis=0)
    input_grad = kernel_call(
        input_terms,
        shape((ROWS, quarter), f32),
        (jnp.stack([c, y]).astype(jnp.int32), terms_x, *w_own, *w_far),
        (),
        2 * ROWS * quarter * xs * 2 * HD,
    )
    parts, input_grad = lax.optimization_barrier((parts, input_grad))
    grads = jnp.sum(parts.astype(f32), 0)
    return (grads[:, :HD], grads[:, HD:], input_grad)


def solution(mesh):
    fine = Mesh(
        mesh.devices.reshape(4, RING // 2, 2, 2, 4), ("y", "zb", "za", "c", "x")
    )
    ctx = ("y", "zb", "za", "c")
    split = P(ctx, "x")
    return jax.shard_map(
        body,
        mesh=fine,
        in_specs=(P(ctx, None), split, split, split, split, split, P(ctx)),
        out_specs=(split, split, split),
        check_vma=False,
    )
```
